32 devices in a mesh: mass: 8 (over z, core), pep: 4 (over y, x).
Axes of the slice: x: 2, y: 2, z: 4, core: 2. Of those that a mesh axis runs over, the one named last changes fastest.
Arguments:
- spectra: bfloat16 [4096, 2048], P('mass'), may hold values from 0 to 2
- peptides: bfloat16 [32768, 2048], P(('mass', 'pep')), may hold values from -0.125 to 0.125
- bounds: int32 [4096, 2], P('mass'), may hold values from 0 to 32767, as said below
Outputs:
- best_score: float32 [4096], P('mass')
The draws below stay inside these ranges and needn't reach their ends.
Inputs may be any that keep to these rules, and one draw needn't show every extreme that they name: For spectrum i in slab s = i // 512: bounds[i, 0] <= bounds[i, 1]; bounds[i, 0] > (s - 1) * 4096 or is 0; bounds[i, 1] < (s + 2) * 4096; the window holds at least one peptide index of slab s, that is of [s * 4096, (s + 1) * 4096).
All inputs are finite; a program needn't handle non-finite values.
Results may differ from the reference program's by a relative error of at most 0.00085.
Values may be sent and summed in bfloat16 or wider, within the bound.
No kernel may reach another device: no remote copies, remote signals or barrier semaphores. Data moves between devices by JAX's collectives and lax.ppermute only.
A program may use at most 64 MiB of HBM per device.

```python
import jax
import jax.numpy as jnp
from jax import lax

BINS = 2048
HALF_TAPS = 75
SPEC_DEV = 512
PEP_DEV = 1024
PEPSLAB = 4096
NSPEC = 4096
NPEP = 32768
N_MASS = 8


def draw_bounds(key, part):
    first_key = jax.random.fold_in(key, 11)
    second_key = jax.random.fold_in(key, 12)
    third_key = jax.random.fold_in(key, 13)
    stride = max(PEPSLAB // SPEC_DEV, 1)
    index = jnp.arange(NSPEC, dtype=jnp.int32)
    slab = index // SPEC_DEV
    local = index % SPEC_DEV
    center = slab * PEPSLAB + local * PEPSLAB // SPEC_DEV + jax.random.randint(first_key, (NSPEC,), 0, stride)
    lower = center - jax.random.randint(second_key, (NSPEC,), PEPSLAB // 4, PEPSLAB)
    upper = center + jax.random.randint(third_key, (NSPEC,), PEPSLAB // 4, PEPSLAB)
    top_rank = SPEC_DEV - 1 - local
    top_edge = top_rank < 3
    lower = jnp.where(top_edge, (slab + 1) * PEPSLAB - 1 - top_rank, lower)
    upper = jnp.where(top_edge, (slab + 1) * PEPSLAB + PEP_DEV - 1, upper)
    bottom_edge = local < 3
    lower = jnp.where(bottom_edge, slab * PEPSLAB - PEP_DEV, lower)
    upper = jnp.where(bottom_edge, slab * PEPSLAB + local, upper)
    lower = jnp.clip(lower, 0, NPEP - 1)
    upper = jnp.clip(upper, 0, NPEP - 1)
    return jnp.stack([lower, upper], axis=1).astype(jnp.int32)


def levels(key, shape, cuts, least, top_value):
    gain = 1.0
    for position, parts in cuts:
        heights = jax.random.uniform(jax.random.fold_in(jax.random.fold_in(key, 6), position), (parts,), jnp.float32, least / len(cuts), top_value / len(cuts))
        gain = gain * jnp.repeat(jnp.exp(heights), shape[position] // parts).reshape((-1,) + (1,) * (len(shape) - 1 - position))
    return gain


def gaussian(key, shape, spread, limit, pieces=(), kind=jnp.bfloat16):
    values = spread * jax.random.normal(key, shape, jnp.float32)
    if pieces:
        values = values * levels(key, shape, pieces, -0.22, 0.18)
    return jnp.clip(values, -limit, limit).astype(kind)


def setup_inputs(seed: int = 0) -> dict:
    splits = jax.random.split(jax.random.key(seed), 4)
    return {
        "spectra": jnp.clip(2.0 * jax.random.uniform(splits[0], (NSPEC, BINS), jnp.float32) ** levels(splits[0], (NSPEC, BINS), ((0, 8),), -0.2, 0.2), 0.0, 2.0).astype(jnp.bfloat16),
        "peptides": gaussian(splits[1], (NPEP, BINS), BINS ** -0.5, 0.125, ((0, 32),)),
        "bounds": draw_bounds(jax.random.fold_in(splits[3], 71), 0),
    }


def process(spectra):
    values = spectra.astype(jnp.float32)
    window_sum = lax.reduce_window(values, jnp.array(0, values.dtype), lax.add, (1, 2 * HALF_TAPS + 1), (1, 1), [(0, 0), (HALF_TAPS, HALF_TAPS)])
    return (values - (window_sum - values) / (2.0 * HALF_TAPS)).astype(jnp.bfloat16)


def reference(spectra, peptides, bounds):
    processed = process(spectra)
    padding = jnp.zeros((PEPSLAB, BINS), peptides.dtype)
    padded = jnp.concatenate([padding, peptides, padding], axis=0)

    def one_slab(slab):
        rows = lax.dynamic_slice_in_dim(processed, slab * SPEC_DEV, SPEC_DEV, 0)
        window = lax.dynamic_slice_in_dim(bounds, slab * SPEC_DEV, SPEC_DEV, 0)
        cands = lax.dynamic_slice_in_dim(padded, slab * PEPSLAB, 3 * PEPSLAB, 0)
        index = ((slab - 1) * PEPSLAB + jnp.arange(3 * PEPSLAB)).astype(jnp.int32)
        score = jnp.dot(rows, cands.T, preferred_element_type=jnp.float32)
        inside = (index[None, :] >= window[:, 0:1]) & (index[None, :] <= window[:, 1:2])
        return jnp.max(jnp.where(inside, score, -1e30), axis=1)

    return lax.map(one_slab, jnp.arange(N_MASS).astype(jnp.int32)).reshape(NSPEC)
```

```python
import functools

import jax
import jax.numpy as jnp
from jax import lax
from jax.experimental import pallas as pl
from jax.experimental.pallas import tpu as pltpu
from jax.sharding import PartitionSpec as P

HALF_TAPS = 75
LOWEST = -1e30
ROW_BY_ROW = (((1,), (1,)), ((), ()))
VMEM = pl.BlockSpec(memory_space=pltpu.VMEM)
SMEM = pl.BlockSpec(memory_space=pltpu.SMEM)
BLOCK = 256
PAD = 128


def process_into(rows_ref, out_ref):
    bins = rows_ref.shape[1]
    source = lax.broadcasted_iota(jnp.int32, (BLOCK + 2 * PAD, BLOCK), 0) - PAD
    target = lax.broadcasted_iota(jnp.int32, (BLOCK + 2 * PAD, BLOCK), 1)
    band = jnp.where(jnp.abs(source - target) <= HALF_TAPS, 1.0, 0.0).astype(jnp.bfloat16)
    for start in range(0, bins, BLOCK):
        low, high = max(start - PAD, 0), min(start + BLOCK + PAD, bins)
        skip = low - (start - PAD)
        window_sum = jnp.dot(
            rows_ref[:, low:high],
            band[skip : skip + high - low],
            preferred_element_type=jnp.float32,
        )
        values = rows_ref[:, start : start + BLOCK].astype(jnp.float32)
        out_ref[:, start : start + BLOCK] = (
            values - (window_sum - values) * (1.0 / (2.0 * HALF_TAPS))
        ).astype(jnp.bfloat16)


def best_of(processed, peptides_ref, bounds, first):
    score = lax.dot_general(
        peptides_ref[...], processed, ROW_BY_ROW, preferred_element_type=jnp.float32
    )
    index = lax.broadcasted_iota(jnp.int32, score.shape, 0)
    inside = (index >= bounds[0:1, :] - first) & (index <= bounds[1:2, :] - first)
    return jnp.max(jnp.where(inside, score, LOWEST), axis=0, keepdims=True)


def score_kernel(place_ref, rows_ref, peptides_ref, bounds_ref, best_ref, processed):
    process_into(rows_ref, processed)
    best_ref[...] = best_of(processed[...], peptides_ref, bounds_ref[...], place_ref[0])


def last_kernel(
    place_ref, rows_ref, peptides_ref, bounds_ref, own_ref, back_ref, out_ref, processed, far
):
    far[...] = jnp.full(far.shape, LOWEST, jnp.float32)

    @pl.when(place_ref[1] > 0)
    def _():
        process_into(rows_ref, processed)
        far[...] = best_of(processed[...], peptides_ref, bounds_ref[...], place_ref[0])

    near = jnp.maximum(own_ref[...], back_ref[...])
    half = (out_ref.shape[0] // 2, out_ref.shape[1])
    lower = place_ref[2] > 0
    out_ref[: half[0]] = jnp.broadcast_to(jnp.where(lower, near, far[...]), half)
    out_ref[half[0] :] = jnp.broadcast_to(jnp.where(lower, far[...], near), half)


def cost(rows, peptides):
    bins = peptides.shape[1]
    return pl.CostEstimate(
        flops=2 * rows * bins * (peptides.shape[0] + BLOCK + 2 * PAD),
        bytes_accessed=2 * bins * (peptides.shape[0] + rows),
        transcendentals=0,
    )


def per_device(spectra, peptides, bounds):
    slabs, shards = lax.axis_size("mass"), lax.axis_size("pep")
    slab, shard = lax.axis_index("mass"), lax.axis_index("pep")
    rows, bins = spectra.shape
    pep_rows = peptides.shape[0]
    chip = [(i, i ^ 1) for i in range(slabs)]
    pairs = [(i, i + 1) for i in range(1, slabs - 1, 2)]
    across = pairs + [(high, low) for low, high in pairs]
    groups = [
        [i * shards + j for i in pair for j in range(shards)]
        for pair in pairs + [(0, slabs - 1)]
    ]
    edge = (slab == 0) | (slab == slabs - 1)
    lower = (slab == 0) | ((slab % 2 == 1) & (slab < slabs - 1))
    place = jnp.stack(
        [(slab * shards + shard) * pep_rows, 1 - edge.astype(jnp.int32), lower.astype(jnp.int32)]
    ).astype(jnp.int32)
    windows = bounds.T

    far_rows = lax.ppermute(spectra, "mass", across)
    far_windows = lax.ppermute(windows, "mass", across)
    near_rows = lax.ppermute(spectra, "mass", chip)
    near_windows = lax.ppermute(windows, "mass", chip)

    score = pl.pallas_call(
        score_kernel,
        out_shape=jax.ShapeDtypeStruct((1, rows), jnp.float32),
        in_specs=[SMEM, VMEM, VMEM, VMEM],
        out_specs=VMEM,
        scratch_shapes=[pltpu.VMEM((rows, bins), jnp.bfloat16)],
        compiler_params=pltpu.CompilerParams(vmem_limit_bytes=16 * 2**20),
        cost_estimate=cost(rows, peptides),
    )
    own = score(place, spectra, peptides, windows)
    near = score(place, near_rows, peptides, near_windows)
    back = lax.ppermute(near, "mass", chip)
    bests = pl.pallas_call(
        last_kernel,
        out_shape=jax.ShapeDtypeStruct((2 * shards, rows), jnp.float32),
        in_specs=[SMEM, VMEM, VMEM, VMEM, VMEM, VMEM],
        out_specs=VMEM,
        scratch_shapes=[
            pltpu.VMEM((rows, bins), jnp.bfloat16),
            pltpu.VMEM((1, rows), jnp.float32),
        ],
        compiler_params=pltpu.CompilerParams(vmem_limit_bytes=16 * 2**20),
        cost_estimate=cost(rows, peptides),
    )(place, far_rows, peptides, far_windows, own, back)
    bests = lax.all_to_all(bests, ("mass", "pep"), 0, 0, axis_index_groups=groups)
    return jnp.max(bests, axis=0)


def solution(mesh):
    in_specs = (P("mass", None), P(("mass", "pep"), None), P("mass", None))
    out_specs = P("mass")
    return jax.shard_map(
        per_device, mesh=mesh, in_specs=in_specs, out_specs=out_specs, check_vma=False
    )
```

```python
import jax
import jax.numpy as jnp
from jax import lax
from jax.experimental import pallas as pl
from jax.experimental.pallas import tpu as pltpu
from jax.sharding import PartitionSpec as P

HALF_TAPS = 75
LOWEST = -1e30
ROW_BY_ROW = (((1,), (1,)), ((), ()))
VMEM = pl.BlockSpec(memory_space=pltpu.VMEM)
SMEM = pl.BlockSpec(memory_space=pltpu.SMEM)
HBM = pl.BlockSpec(memory_space=pltpu.HBM)
BLOCK = 256
PAD = 128
NOTE = 16
LONG = 2**35
DIGITS = 3


def process_into(rows_ref, out_ref):
    bins = rows_ref.shape[1]
    source = lax.broadcasted_iota(jnp.int32, (BLOCK + 2 * PAD, BLOCK), 0) - PAD
    target = lax.broadcasted_iota(jnp.int32, (BLOCK + 2 * PAD, BLOCK), 1)
    band = jnp.where(jnp.abs(source - target) <= HALF_TAPS, 1.0, 0.0).astype(jnp.bfloat16)
    for start in range(0, bins, BLOCK):
        low, high = max(start - PAD, 0), min(start + BLOCK + PAD, bins)
        skip = low - (start - PAD)
        window_sum = jnp.dot(
            rows_ref[:, low:high],
            band[skip : skip + high - low],
            preferred_element_type=jnp.float32,
        )
        values = rows_ref[:, start : start + BLOCK].astype(jnp.float32)
        out_ref[:, start : start + BLOCK] = (
            values - (window_sum - values) * (1.0 / (2.0 * HALF_TAPS))
        ).astype(jnp.bfloat16)


def best_of(processed, peptides, bounds, first):
    score = lax.dot_general(peptides, processed, ROW_BY_ROW, preferred_element_type=jnp.float32)
    index = lax.broadcasted_iota(jnp.int32, score.shape, 0)
    inside = (index >= bounds[0] - first) & (index <= bounds[1] - first)
    return jnp.max(jnp.where(inside, score, LOWEST), axis=0, keepdims=True)


def write_note(note_ref, bounds_ref):
    rows = bounds_ref.shape[1]
    row = lax.broadcasted_iota(jnp.int32, (NOTE, rows), 0)
    note = jnp.zeros((NOTE, rows), jnp.int32)
    for k in range(2):
        for d in range(DIGITS):
            digit = (bounds_ref[k : k + 1, :] >> (8 * d)) & 255
            note = jnp.where(row == k * DIGITS + d, digit, note)
    note_ref[...] = jnp.zeros(note_ref.shape, note_ref.dtype)
    note_ref[:, :rows] = note.astype(jnp.float32).astype(note_ref.dtype)


def read_note(note_ref, rows):
    note = note_ref[:, :rows].astype(jnp.float32).astype(jnp.int32)
    return [
        sum(note[k * DIGITS + d : k * DIGITS + d + 1, :] << (8 * d) for d in range(DIGITS))
        for k in range(2)
    ]


def quarter_kernel(place_ref, spectra_ref, quarter_ref, sem):
    part = quarter_ref.shape[0]
    start = pl.multiple_of(place_ref[3] * (spectra_ref.shape[0] - part), 16)
    copy = pltpu.make_async_copy(spectra_ref.at[pl.ds(start, part)], quarter_ref, sem)
    copy.start()
    copy.wait()


def prepare_kernel(
    spectra_ref, bounds_ref, peptides_ref, middle_ref, whole_ref, held_ref, raw, windows, sems
):
    rows = spectra_ref.shape[0]
    half = rows // 2
    count = middle_ref.shape[0] - NOTE
    part = (rows - count) // 2
    sources = [
        (spectra_ref.at[:half], raw.at[:half]),
        (spectra_ref.at[half:], raw.at[half:]),
        (bounds_ref, windows),
        (spectra_ref.at[part : part + count], middle_ref.at[:count]),
        (peptides_ref, held_ref),
    ]
    copies = [
        pltpu.make_async_copy(source, target, sems.at[i])
        for i, (source, target) in enumerate(sources)
    ]
    for copy in copies:
        copy.start()
    copies[0].wait()
    process_into(raw.at[:half], whole_ref.at[:half])
    copies[1].wait()
    process_into(raw.at[half:], whole_ref.at[half:rows])
    copies[2].wait()
    write_note(whole_ref.at[rows:], windows)
    write_note(middle_ref.at[count:], windows)
    copies[3].wait()
    copies[4].wait()


def near_kernel(place_ref, whole_ref, peptides_ref, best_ref):
    rows = best_ref.shape[1]
    bounds = read_note(whole_ref.at[rows:], rows)
    best_ref[...] = best_of(whole_ref[:rows, :], peptides_ref[...], bounds, place_ref[0])


def process_kernel(rows_ref, processed_ref):
    process_into(rows_ref, processed_ref)


def last_kernel(
    place_ref,
    direct_ref,
    relayed_ref,
    far_ref,
    peptides_ref,
    own_ref,
    back_ref,
    out_ref,
    processed,
    far_best,
):
    part = direct_ref.shape[0]
    rows = own_ref.shape[1]
    far_best[...] = jnp.full(far_best.shape, LOWEST, jnp.float32)

    @pl.when(place_ref[1] > 0)
    def _():
        odd = place_ref[3]
        start = pl.multiple_of(odd * (rows - part), part)
        other = pl.multiple_of((1 - odd) * (rows - part), part)
        processed[pl.ds(start, part), :] = direct_ref[...]
        process_into(relayed_ref, processed.at[pl.ds(other, part)])
        process_into(far_ref.at[: rows - 2 * part], processed.at[part : rows - part])
        bounds = read_note(far_ref.at[rows - 2 * part :], rows)
        far_best[...] = best_of(processed[...], peptides_ref[...], bounds, place_ref[0])

    near = jnp.maximum(own_ref[...], back_ref[...])
    half = (out_ref.shape[0] // 2, rows)
    lower = place_ref[2] > 0
    out_ref[: half[0]] = jnp.broadcast_to(jnp.where(lower, near, far_best[...]), half)
    out_ref[half[0] :] = jnp.broadcast_to(jnp.where(lower, far_best[...], near), half)


def in_hbm(array):
    return pltpu.with_memory_space_constraint(array, pltpu.HBM)


def call(kernel, out_shapes, in_specs, scratch, flops=1024):
    return pl.pallas_call(
        kernel,
        out_shape=[jax.ShapeDtypeStruct(shape, dtype) for shape, dtype in out_shapes],
        in_specs=in_specs,
        out_specs=[VMEM] * len(out_shapes),
        scratch_shapes=scratch,
        compiler_params=pltpu.CompilerParams(vmem_limit_bytes=20 * 2**20),
        cost_estimate=pl.CostEstimate(flops=flops, bytes_accessed=1024, transcendentals=0),
    )


def per_device(spectra, peptides, bounds):
    slabs, shards = lax.axis_size("mass"), lax.axis_size("pep")
    slab, shard = lax.axis_index("mass"), lax.axis_index("pep")
    rows, bins = spectra.shape
    pep_rows = peptides.shape[0]
    part = rows // 4
    bf16, f32 = jnp.bfloat16, jnp.float32
    chip = [(i, i ^ 1) for i in range(slabs)]
    pairs = [(i, i + 1) for i in range(1, slabs - 1, 2)]
    across = pairs + [(high, low) for low, high in pairs]
    groups = [
        [i * shards + j for i in pair for j in range(shards)]
        for pair in pairs + [(0, slabs - 1)]
    ]
    beside = (1, shards // 2)
    relay = [
        (i * shards + j, i * shards + (j ^ beside[i % 2]))
        for i in range(1, slabs - 1)
        for j in range(shards)
    ]
    odd = (shard // beside[0] + shard // beside[1]) % 2
    edge = (slab == 0) | (slab == slabs - 1)
    lower = (slab == 0) | ((slab % 2 == 1) & (slab < slabs - 1))
    place = jnp.stack(
        [
            (slab * shards + shard) * pep_rows,
            1 - edge.astype(jnp.int32),
            lower.astype(jnp.int32),
            odd,
        ]
    ).astype(jnp.int32)
    windows = bounds.T

    spectra, windows, peptides = in_hbm(spectra), in_hbm(windows), in_hbm(peptides)

    (quarter,) = call(
        quarter_kernel,
        [((part, bins), bf16)],
        [SMEM, HBM],
        [pltpu.SemaphoreType.DMA],
    )(place, spectra)
    direct = lax.ppermute(quarter, "mass", across)

    quarter, windows = lax.optimization_barrier((quarter, windows))
    middle, whole, held = call(
        prepare_kernel,
        [
            ((rows - 2 * part + NOTE, bins), bf16),
            ((rows + NOTE, bins), bf16),
            (peptides.shape, bf16),
        ],
        [HBM, HBM, HBM],
        [
            pltpu.VMEM((rows, bins), bf16),
            pltpu.VMEM(windows.shape, jnp.int32),
            pltpu.SemaphoreType.DMA((5,)),
        ],
    )(spectra, in_hbm(windows), peptides)
    far = lax.ppermute(middle, "mass", across)
    score = [((1, rows), f32)], [SMEM, VMEM, VMEM], []
    (own_best,) = call(near_kernel, *score)(place, whole, held)

    direct, whole, own_best = lax.optimization_barrier((direct, whole, own_best))
    near = lax.ppermute(whole, "mass", chip)
    relayed = lax.ppermute(direct, ("mass", "pep"), relay)
    (direct,) = call(process_kernel, [((part, bins), bf16)], [VMEM], [], LONG)(direct)
    near, direct = lax.optimization_barrier((near, direct))
    (near_best,) = call(near_kernel, *score)(place, near, held)
    back = lax.ppermute(near_best, "mass", chip)

    (bests,) = call(
        last_kernel,
        [((2 * shards, rows), f32)],
        [SMEM] + [VMEM] * 6,
        [pltpu.VMEM((rows, bins), bf16), pltpu.VMEM((1, rows), f32)],
    )(place, direct, relayed, far, held, own_best, back)
    bests = lax.all_to_all(bests, ("mass", "pep"), 0, 0, axis_index_groups=groups)
    return jnp.max(bests, axis=0)


def solution(mesh):
    in_specs = (P("mass", None), P(("mass", "pep"), None), P("mass", None))
    out_specs = P("mass")
    return jax.shard_map(
        per_device, mesh=mesh, in_specs=in_specs, out_specs=out_specs, check_vma=False
    )
```

```python
import jax
import jax.numpy as jnp
from jax import lax
from jax.experimental import pallas as pl
from jax.experimental.pallas import tpu as pltpu
from jax.sharding import PartitionSpec as P

HALF_TAPS = 75
LOWEST = -1e30
ROW_BY_ROW = (((1,), (1,)), ((), ()))
VMEM = pl.BlockSpec(memory_space=pltpu.VMEM)
HBM = pl.BlockSpec(memory_space=pltpu.HBM)
BLOCK = 256
PAD = 128
NOTE = 16
LONG = 2**35
DIGITS = 3


def beside(shards):
    return 1, shards // 2


def place(peptides_ref):
    slabs, shards = lax.axis_size("mass"), lax.axis_size("pep")
    slab, shard = lax.axis_index("mass"), lax.axis_index("pep")
    inner = (slab > 0) & (slab < slabs - 1)
    lower = (slab == 0) | ((slab % 2 == 1) & inner)
    odd = (shard // beside(shards)[0] + shard // beside(shards)[1]) % 2
    return (slab * shards + shard) * peptides_ref.shape[0], inner, lower, odd


def process_into(rows_ref, out_ref):
    bins = rows_ref.shape[1]
    source = lax.broadcasted_iota(jnp.int32, (BLOCK + 2 * PAD, BLOCK), 0) - PAD
    target = lax.broadcasted_iota(jnp.int32, (BLOCK + 2 * PAD, BLOCK), 1)
    band = jnp.where(jnp.abs(source - target) <= HALF_TAPS, 1.0, 0.0).astype(jnp.bfloat16)
    for start in range(0, bins, BLOCK):
        low, high = max(start - PAD, 0), min(start + BLOCK + PAD, bins)
        skip = low - (start - PAD)
        window_sum = jnp.dot(
            rows_ref[:, low:high],
            band[skip : skip + high - low],
            preferred_element_type=jnp.float32,
        )
        values = rows_ref[:, start : start + BLOCK].astype(jnp.float32)
        out_ref[:, start : start + BLOCK] = (
            values - (window_sum - values) * (1.0 / (2.0 * HALF_TAPS))
        ).astype(jnp.bfloat16)


def best_of(processed, peptides, bounds, first):
    score = lax.dot_general(peptides, processed, ROW_BY_ROW, preferred_element_type=jnp.float32)
    index = lax.broadcasted_iota(jnp.int32, score.shape, 0)
    inside = (index >= bounds[0] - first) & (index <= bounds[1] - first)
    return jnp.max(jnp.where(inside, score, LOWEST), axis=0, keepdims=True)


def write_note(note_ref, bounds_ref):
    rows = bounds_ref.shape[1]
    row = lax.broadcasted_iota(jnp.int32, (NOTE, rows), 0)
    note = jnp.zeros((NOTE, rows), jnp.int32)
    for k in range(2):
        for d in range(DIGITS):
            digit = (bounds_ref[k : k + 1, :] >> (8 * d)) & 255
            note = jnp.where(row == k * DIGITS + d, digit, note)
    note_ref[...] = jnp.zeros(note_ref.shape, note_ref.dtype)
    note_ref[:, :rows] = note.astype(jnp.float32).astype(note_ref.dtype)


def read_note(note_ref, rows):
    note = note_ref[:, :rows].astype(jnp.float32).astype(jnp.int32)
    return [
        sum(note[k * DIGITS + d : k * DIGITS + d + 1, :] << (8 * d) for d in range(DIGITS))
        for k in range(2)
    ]


def quarter_kernel(spectra_ref, quarter_ref, raw, sems):
    part = quarter_ref.shape[0]
    start = place(spectra_ref)[3] * (spectra_ref.shape[0] - part)
    step = part // sems.shape[0]
    cuts = [(i * step, step) for i in range(sems.shape[0])]
    copies = [
        pltpu.make_async_copy(
            spectra_ref.at[pl.ds(pl.multiple_of(start + low, 16), size)],
            raw.at[low : low + size],
            sems.at[i],
        )
        for i, (low, size) in enumerate(cuts)
    ]
    for copy in copies:
        copy.start()
    for copy in copies:
        copy.wait()
    process_into(raw, quarter_ref)


def middle_kernel(spectra_ref, bounds_ref, middle_ref, raw, windows, sems):
    count = raw.shape[0]
    part = (spectra_ref.shape[0] - count) // 2
    rows = pltpu.make_async_copy(spectra_ref.at[part : part + count], raw, sems.at[0])
    bounds = pltpu.make_async_copy(bounds_ref, windows, sems.at[1])
    bounds.start()
    rows.start()
    bounds.wait()
    write_note(middle_ref.at[count:], windows)
    rows.wait()
    process_into(raw, middle_ref.at[:count])


def whole_kernel(
    spectra_ref, peptides_ref, quarter_ref, middle_ref, whole_ref, held_ref, raw, sems
):
    rows = spectra_ref.shape[0]
    part = quarter_ref.shape[0]
    odd = place(held_ref)[3]
    start = pl.multiple_of(odd * (rows - part), 16)
    other = pl.multiple_of((1 - odd) * (rows - part), 16)
    rest = pltpu.make_async_copy(spectra_ref.at[pl.ds(other, part)], raw, sems.at[0])
    peptides = pltpu.make_async_copy(peptides_ref, held_ref, sems.at[1])
    rest.start()
    peptides.start()
    whole_ref[pl.ds(start, part), :] = quarter_ref[...]
    whole_ref[part : rows - part, :] = middle_ref[: rows - 2 * part, :]
    whole_ref[rows:, :] = middle_ref[rows - 2 * part :, :]
    rest.wait()
    process_into(raw, whole_ref.at[pl.ds(other, part)])
    peptides.wait()


def near_kernel(whole_ref, peptides_ref, best_ref):
    rows = best_ref.shape[1]
    bounds = read_note(whole_ref.at[rows:], rows)
    best_ref[...] = best_of(whole_ref[:rows, :], peptides_ref[...], bounds, place(peptides_ref)[0])


def last_kernel(
    direct_ref,
    relayed_ref,
    middle_ref,
    peptides_ref,
    own_ref,
    back_ref,
    out_ref,
    outer,
    far_best,
):
    part = direct_ref.shape[0]
    rows = own_ref.shape[1]
    far_best[...] = jnp.full(far_best.shape, LOWEST, jnp.float32)

    @pl.when(place(peptides_ref)[1])
    def _():
        odd = place(peptides_ref)[3]
        outer[pl.ds(pl.multiple_of(odd * part, 16), part), :] = direct_ref[...]
        outer[pl.ds(pl.multiple_of((1 - odd) * part, 16), part), :] = relayed_ref[...]
        count = rows - 2 * part
        bounds = read_note(middle_ref.at[count:], rows)
        first = place(peptides_ref)[0]
        far_best[:, part : part + count] = best_of(
            middle_ref[:count, :],
            peptides_ref[...],
            [bound[:, part : part + count] for bound in bounds],
            first,
        )
        ends = [
            jnp.concatenate([bound[:, :part], bound[:, part + count :]], axis=1)
            for bound in bounds
        ]
        best = best_of(outer[...], peptides_ref[...], ends, first)
        far_best[:, :part] = best[:, :part]
        far_best[:, part + count :] = best[:, part:]

    near = jnp.maximum(own_ref[...], back_ref[...])
    half = (out_ref.shape[0] // 2, rows)
    lower = place(peptides_ref)[2]
    out_ref[: half[0]] = jnp.broadcast_to(jnp.where(lower, near, far_best[...]), half)
    out_ref[half[0] :] = jnp.broadcast_to(jnp.where(lower, far_best[...], near), half)


def in_hbm(array):
    return pltpu.with_memory_space_constraint(array, pltpu.HBM)


def call(kernel, out_shapes, in_specs, scratch, flops=1024):
    return pl.pallas_call(
        kernel,
        out_shape=[jax.ShapeDtypeStruct(shape, dtype) for shape, dtype in out_shapes],
        in_specs=in_specs,
        out_specs=[VMEM] * len(out_shapes),
        scratch_shapes=scratch,
        compiler_params=pltpu.CompilerParams(vmem_limit_bytes=20 * 2**20),
        cost_estimate=pl.CostEstimate(flops=flops, bytes_accessed=1024, transcendentals=0),
    )


def per_device(spectra, peptides, bounds):
    slabs, shards = lax.axis_size("mass"), lax.axis_size("pep")
    rows, bins = spectra.shape
    pep_rows = peptides.shape[0]
    part = rows // 4
    bf16, f32 = jnp.bfloat16, jnp.float32
    chip = [(i, i ^ 1) for i in range(slabs)]
    pairs = [(i, i + 1) for i in range(1, slabs - 1, 2)]
    across = pairs + [(high, low) for low, high in pairs]
    groups = [
        [i * shards + j for i in pair for j in range(shards)]
        for pair in pairs + [(0, slabs - 1)]
    ]
    relay = [
        (i * shards + j, i * shards + (j ^ beside(shards)[i % 2]))
        for i in range(1, slabs - 1)
        for j in range(shards)
    ]
    windows = bounds.T

    spectra, windows, peptides = in_hbm(spectra), in_hbm(windows), in_hbm(peptides)

    (quarter,) = call(
        quarter_kernel,
        [((part, bins), bf16)],
        [HBM],
        [pltpu.VMEM((part, bins), bf16), pltpu.SemaphoreType.DMA((2,))],
    )(spectra)
    direct = lax.ppermute(quarter, "mass", across)

    quarter, windows = lax.optimization_barrier((quarter, windows))
    (middle,) = call(
        middle_kernel,
        [((rows - 2 * part + NOTE, bins), bf16)],
        [HBM, HBM],
        [
            pltpu.VMEM((rows - 2 * part, bins), bf16),
            pltpu.VMEM(windows.shape, jnp.int32),
            pltpu.SemaphoreType.DMA((2,)),
        ],
    )(spectra, in_hbm(windows))
    far = lax.ppermute(middle, "mass", across)
    whole, held = call(
        whole_kernel,
        [((rows + NOTE, bins), bf16), (peptides.shape, bf16)],
        [HBM, HBM, VMEM, VMEM],
        [pltpu.VMEM((part, bins), bf16), pltpu.SemaphoreType.DMA((2,))],
    )(spectra, peptides, quarter, middle)

    score = [((1, rows), f32)], [VMEM, VMEM], []
    (own_best,) = call(near_kernel, *score, LONG)(whole, held)
    direct, whole = lax.optimization_barrier((direct, whole))
    near = lax.ppermute(whole, "mass", chip)
    relayed = lax.ppermute(direct, ("mass", "pep"), relay)
    near, own_best = lax.optimization_barrier((near, own_best))
    (near_best,) = call(near_kernel, *score)(near, held)
    back = lax.ppermute(near_best, "mass", chip)

    (bests,) = call(
        last_kernel,
        [((2 * shards, rows), f32)],
        [VMEM] * 6,
        [pltpu.VMEM((2 * part, bins), bf16), pltpu.VMEM((1, rows), f32)],
    )(direct, relayed, far, held, own_best, back)
    bests = lax.all_to_all(bests, ("mass", "pep"), 0, 0, axis_index_groups=groups)
    return jnp.max(bests, axis=0)


def solution(mesh):
    in_specs = (P("mass", None), P(("mass", "pep"), None), P("mass", None))
    out_specs = P("mass")
    return jax.shard_map(
        per_device, mesh=mesh, in_specs=in_specs, out_specs=out_specs, check_vma=False
    )
```

```python
import jax
import jax.numpy as jnp
from jax import lax
from jax.experimental import pallas as pl
from jax.experimental.pallas import tpu as pltpu
from jax.sharding import PartitionSpec as P

HALF_TAPS = 75
LOWEST = -1e30
ROW_BY_ROW = (((1,), (1,)), ((), ()))
VMEM = pl.BlockSpec(memory_space=pltpu.VMEM)
HBM = pl.BlockSpec(memory_space=pltpu.HBM)
BLOCK = 256
PAD = 128
NOTE = 8
LONG = 2**35
DIGITS = 3


def beside(shards):
    return 1, shards // 2


def place(peptides_ref):
    slabs, shards = lax.axis_size("mass"), lax.axis_size("pep")
    slab, shard = lax.axis_index("mass"), lax.axis_index("pep")
    inner = (slab > 0) & (slab < slabs - 1)
    lower = (slab == 0) | ((slab % 2 == 1) & inner)
    odd = (shard // beside(shards)[0] + shard // beside(shards)[1]) % 2
    return (slab * shards + shard) * peptides_ref.shape[0], inner, lower, odd


def process_into(rows_ref, out_ref):
    bins = rows_ref.shape[1]
    source = lax.broadcasted_iota(jnp.int32, (BLOCK + 2 * PAD, BLOCK), 0) - PAD
    target = lax.broadcasted_iota(jnp.int32, (BLOCK + 2 * PAD, BLOCK), 1)
    band = jnp.where(jnp.abs(source - target) <= HALF_TAPS, 1.0, 0.0).astype(jnp.bfloat16)
    for start in range(0, bins, BLOCK):
        low, high = max(start - PAD, 0), min(start + BLOCK + PAD, bins)
        skip = low - (start - PAD)
        window_sum = jnp.dot(
            rows_ref[:, low:high],
            band[skip : skip + high - low],
            preferred_element_type=jnp.float32,
        )
        values = rows_ref[:, start : start + BLOCK].astype(jnp.float32)
        out_ref[:, start : start + BLOCK] = (
            values - (window_sum - values) * (1.0 / (2.0 * HALF_TAPS))
        ).astype(jnp.bfloat16)


def best_of(processed, peptides, bounds, first):
    score = lax.dot_general(peptides, processed, ROW_BY_ROW, preferred_element_type=jnp.float32)
    index = lax.broadcasted_iota(jnp.int32, score.shape, 0)
    inside = (index >= bounds[0] - first) & (index <= bounds[1] - first)
    return jnp.max(jnp.where(inside, score, LOWEST), axis=0, keepdims=True)


def write_note(note_ref, bounds_ref):
    rows = bounds_ref.shape[1]
    row = lax.broadcasted_iota(jnp.int32, (NOTE, rows), 0)
    note = jnp.zeros((NOTE, rows), jnp.int32)
    for k in range(2):
        for d in range(DIGITS):
            digit = (bounds_ref[k : k + 1, :] >> (8 * d)) & 255
            note = jnp.where(row == k * DIGITS + d, digit, note)
    note_ref[...] = jnp.zeros(note_ref.shape, note_ref.dtype)
    note_ref[:, :rows] = note.astype(jnp.float32).astype(note_ref.dtype)


def read_note(note_ref, rows):
    note = note_ref[:, :rows].astype(jnp.float32).astype(jnp.int32)
    return [
        sum(note[k * DIGITS + d : k * DIGITS + d + 1, :] << (8 * d) for d in range(DIGITS))
        for k in range(2)
    ]


def quarter_kernel(spectra_ref, quarter_ref, raw, sems):
    part = quarter_ref.shape[0]
    start = place(spectra_ref)[3] * (spectra_ref.shape[0] - part)
    step = part // sems.shape[0]
    cuts = [(i * step, step) for i in range(sems.shape[0])]
    copies = [
        pltpu.make_async_copy(
            spectra_ref.at[pl.ds(pl.multiple_of(start + low, 16), size)],
            raw.at[low : low + size],
            sems.at[i],
        )
        for i, (low, size) in enumerate(cuts)
    ]
    for copy in copies:
        copy.start()
    for copy in copies:
        copy.wait()
    process_into(raw, quarter_ref)


def middle_kernel(spectra_ref, bounds_ref, middle_ref, raw, windows, sems):
    count = raw.shape[0]
    part = (spectra_ref.shape[0] - count) // 2
    rows = pltpu.make_async_copy(spectra_ref.at[part : part + count], raw, sems.at[0])
    bounds = pltpu.make_async_copy(bounds_ref, windows, sems.at[1])
    bounds.start()
    rows.start()
    bounds.wait()
    write_note(middle_ref.at[count:], windows)
    rows.wait()
    process_into(raw, middle_ref.at[:count])


def whole_kernel(
    spectra_ref, peptides_ref, quarter_ref, middle_ref, whole_ref, held_ref, raw, sems
):
    rows = spectra_ref.shape[0]
    part = quarter_ref.shape[0]
    odd = place(held_ref)[3]
    start = pl.multiple_of(odd * (rows - part), 16)
    other = pl.multiple_of((1 - odd) * (rows - part), 16)
    rest = pltpu.make_async_copy(spectra_ref.at[pl.ds(other, part)], raw, sems.at[0])
    peptides = pltpu.make_async_copy(peptides_ref, held_ref, sems.at[1])
    rest.start()
    peptides.start()
    whole_ref[pl.ds(start, part), :] = quarter_ref[...]
    whole_ref[part : rows - part, :] = middle_ref[: rows - 2 * part, :]
    whole_ref[rows:, :] = middle_ref[rows - 2 * part :, :]
    rest.wait()
    process_into(raw, whole_ref.at[pl.ds(other, part)])
    peptides.wait()


def near_kernel(whole_ref, peptides_ref, best_ref):
    rows = best_ref.shape[1]
    bounds = read_note(whole_ref.at[rows:], rows)
    best_ref[...] = best_of(whole_ref[:rows, :], peptides_ref[...], bounds, place(peptides_ref)[0])


def last_kernel(
    direct_ref,
    relayed_ref,
    middle_ref,
    peptides_ref,
    own_ref,
    back_ref,
    out_ref,
    outer,
    far_best,
):
    part = direct_ref.shape[0]
    rows = own_ref.shape[1]
    far_best[...] = jnp.full(far_best.shape, LOWEST, jnp.float32)

    @pl.when(place(peptides_ref)[1])
    def _():
        odd = place(peptides_ref)[3]
        outer[pl.ds(pl.multiple_of(odd * part, 16), part), :] = direct_ref[...]
        outer[pl.ds(pl.multiple_of((1 - odd) * part, 16), part), :] = relayed_ref[...]
        count = rows - 2 * part
        bounds = read_note(middle_ref.at[count:], rows)
        first = place(peptides_ref)[0]
        far_best[:, part : part + count] = best_of(
            middle_ref[:count, :],
            peptides_ref[...],
            [bound[:, part : part + count] for bound in bounds],
            first,
        )
        ends = [
            jnp.concatenate([bound[:, :part], bound[:, part + count :]], axis=1)
            for bound in bounds
        ]
        best = best_of(outer[...], peptides_ref[...], ends, first)
        far_best[:, :part] = best[:, :part]
        far_best[:, part + count :] = best[:, part:]

    near = jnp.maximum(own_ref[...], back_ref[...])
    half = (out_ref.shape[0] // 2, rows)
    lower = place(peptides_ref)[2]
    out_ref[: half[0]] = jnp.broadcast_to(jnp.where(lower, near, far_best[...]), half)
    out_ref[half[0] :] = jnp.broadcast_to(jnp.where(lower, far_best[...], near), half)


def in_hbm(array):
    return pltpu.with_memory_space_constraint(array, pltpu.HBM)


def call(kernel, out_shapes, in_specs, scratch, flops=1024):
    return pl.pallas_call(
        kernel,
        out_shape=[jax.ShapeDtypeStruct(shape, dtype) for shape, dtype in out_shapes],
        in_specs=in_specs,
        out_specs=[VMEM] * len(out_shapes),
        scratch_shapes=scratch,
        compiler_params=pltpu.CompilerParams(vmem_limit_bytes=20 * 2**20),
        cost_estimate=pl.CostEstimate(flops=flops, bytes_accessed=1024, transcendentals=0),
    )


def per_device(spectra, peptides, bounds):
    slabs, shards = lax.axis_size("mass"), lax.axis_size("pep")
    rows, bins = spectra.shape
    pep_rows = peptides.shape[0]
    part = rows // 4
    bf16, f32 = jnp.bfloat16, jnp.float32
    chip = [(i, i ^ 1) for i in range(slabs)]
    pairs = [(i, i + 1) for i in range(1, slabs - 1, 2)]
    across = pairs + [(high, low) for low, high in pairs]
    groups = [
        [i * shards + j for i in pair for j in range(shards)]
        for pair in pairs + [(0, slabs - 1)]
    ]
    relay = [
        (i * shards + j, i * shards + (j ^ beside(shards)[i % 2]))
        for i in range(1, slabs - 1)
        for j in range(shards)
    ]
    windows = bounds.T

    spectra, windows, peptides = in_hbm(spectra), in_hbm(windows), in_hbm(peptides)

    (quarter,) = call(
        quarter_kernel,
        [((part, bins), bf16)],
        [HBM],
        [pltpu.VMEM((part, bins), bf16), pltpu.SemaphoreType.DMA((2,))],
    )(spectra)
    direct = lax.ppermute(quarter, "mass", across)

    quarter, windows = lax.optimization_barrier((quarter, windows))
    (middle,) = call(
        middle_kernel,
        [((rows - 2 * part + NOTE, bins), bf16)],
        [HBM, HBM],
        [
            pltpu.VMEM((rows - 2 * part, bins), bf16),
            pltpu.VMEM(windows.shape, jnp.int32),
            pltpu.SemaphoreType.DMA((2,)),
        ],
    )(spectra, in_hbm(windows))
    far = lax.ppermute(middle, "mass", across)
    whole, held = call(
        whole_kernel,
        [((rows + NOTE, bins), bf16), (peptides.shape, bf16)],
        [HBM, HBM, VMEM, VMEM],
        [pltpu.VMEM((part, bins), bf16), pltpu.SemaphoreType.DMA((2,))],
    )(spectra, peptides, quarter, middle)

    score = [((1, rows), f32)], [VMEM, VMEM], []
    (own_best,) = call(near_kernel, *score, LONG)(whole, held)
    direct, whole = lax.optimization_barrier((direct, whole))
    near = lax.ppermute(whole, "mass", chip)
    relayed = lax.ppermute(direct, ("mass", "pep"), relay)
    near, own_best = lax.optimization_barrier((near, own_best))
    (near_best,) = call(near_kernel, *score)(near, held)
    back = lax.ppermute(near_best, "mass", chip)

    (bests,) = call(
        last_kernel,
        [((2 * shards, rows), f32)],
        [VMEM] * 6,
        [pltpu.VMEM((2 * part, bins), bf16), pltpu.VMEM((1, rows), f32)],
    )(direct, relayed, far, held, own_best, back)
    bests = lax.all_to_all(bests, ("mass", "pep"), 0, 0, axis_index_groups=groups)
    return jnp.max(bests, axis=0)


def solution(mesh):
    in_specs = (P("mass", None), P(("mass", "pep"), None), P("mass", None))
    out_specs = P("mass")
    return jax.shard_map(
        per_device, mesh=mesh, in_specs=in_specs, out_specs=out_specs, check_vma=False
    )
```

```python
import jax
import jax.numpy as jnp
from jax import lax
from jax.experimental import pallas as pl
from jax.experimental.pallas import tpu as pltpu
from jax.sharding import PartitionSpec as P

HALF_TAPS = 75
LOWEST = -1e30
ROW_BY_ROW = (((1,), (1,)), ((), ()))
VMEM = pl.BlockSpec(memory_space=pltpu.VMEM)
HBM = pl.BlockSpec(memory_space=pltpu.HBM)
BLOCK = 256
PAD = 128
NOTE = 16
LONG = 2**35
DIGITS = 3


def beside(shards):
    return 1, shards // 2


def place(peptides_ref):
    slabs, shards = lax.axis_size("mass"), lax.axis_size("pep")
    slab, shard = lax.axis_index("mass"), lax.axis_index("pep")
    inner = (slab > 0) & (slab < slabs - 1)
    lower = (slab == 0) | ((slab % 2 == 1) & inner)
    odd = (shard // beside(shards)[0] + shard // beside(shards)[1]) % 2
    return (slab * shards + shard) * peptides_ref.shape[0], inner, lower, odd


def process_into(rows_ref, out_ref):
    bins = rows_ref.shape[1]
    source = lax.broadcasted_iota(jnp.int32, (BLOCK + 2 * PAD, BLOCK), 0) - PAD
    target = lax.broadcasted_iota(jnp.int32, (BLOCK + 2 * PAD, BLOCK), 1)
    band = jnp.where(jnp.abs(source - target) <= HALF_TAPS, 1.0, 0.0).astype(jnp.bfloat16)
    for start in range(0, bins, BLOCK):
        low, high = max(start - PAD, 0), min(start + BLOCK + PAD, bins)
        skip = low - (start - PAD)
        window_sum = jnp.dot(
            rows_ref[:, low:high],
            band[skip : skip + high - low],
            preferred_element_type=jnp.float32,
        )
        values = rows_ref[:, start : start + BLOCK].astype(jnp.float32)
        out_ref[:, start : start + BLOCK] = (
            values - (window_sum - values) * (1.0 / (2.0 * HALF_TAPS))
        ).astype(jnp.bfloat16)


def best_of(processed, peptides, bounds, first):
    score = lax.dot_general(peptides, processed, ROW_BY_ROW, preferred_element_type=jnp.float32)
    index = lax.broadcasted_iota(jnp.int32, score.shape, 0)
    inside = (index >= bounds[0] - first) & (index <= bounds[1] - first)
    return jnp.max(jnp.where(inside, score, LOWEST), axis=0, keepdims=True)


def meets(bounds, peptides_ref):
    first = place(peptides_ref)[0]
    inside = (bounds[0] < first + peptides_ref.shape[0]) & (bounds[1] >= first)
    return jnp.max(inside.astype(jnp.int32)) > 0


def write_note(note_ref, bounds_ref):
    rows = bounds_ref.shape[1]
    row = lax.broadcasted_iota(jnp.int32, (NOTE, rows), 0)
    note = jnp.zeros((NOTE, rows), jnp.int32)
    for k in range(2):
        for d in range(DIGITS):
            digit = (bounds_ref[k : k + 1, :] >> (8 * d)) & 255
            note = jnp.where(row == k * DIGITS + d, digit, note)
    note_ref[...] = jnp.zeros(note_ref.shape, note_ref.dtype)
    note_ref[:, :rows] = note.astype(jnp.float32).astype(note_ref.dtype)


def read_note(note_ref, rows):
    note = note_ref[:, :rows].astype(jnp.float32).astype(jnp.int32)
    return [
        sum(note[k * DIGITS + d : k * DIGITS + d + 1, :] << (8 * d) for d in range(DIGITS))
        for k in range(2)
    ]


def quarter_kernel(spectra_ref, quarter_ref, raw, sems):
    part = quarter_ref.shape[0]
    start = place(spectra_ref)[3] * (spectra_ref.shape[0] - part)
    step = part // sems.shape[0]
    cuts = [(i * step, step) for i in range(sems.shape[0])]
    copies = [
        pltpu.make_async_copy(
            spectra_ref.at[pl.ds(pl.multiple_of(start + low, 16), size)],
            raw.at[low : low + size],
            sems.at[i],
        )
        for i, (low, size) in enumerate(cuts)
    ]
    for copy in copies:
        copy.start()
    for copy in copies:
        copy.wait()
    process_into(raw, quarter_ref)


def middle_kernel(spectra_ref, bounds_ref, middle_ref, raw, windows, sems):
    count = raw.shape[0]
    part = (spectra_ref.shape[0] - count) // 2
    rows = pltpu.make_async_copy(spectra_ref.at[part : part + count], raw, sems.at[0])
    bounds = pltpu.make_async_copy(bounds_ref, windows, sems.at[1])
    bounds.start()
    rows.start()
    bounds.wait()
    write_note(middle_ref.at[count:], windows)
    rows.wait()
    process_into(raw, middle_ref.at[:count])


def whole_kernel(
    spectra_ref, peptides_ref, quarter_ref, middle_ref, whole_ref, held_ref, raw, sems
):
    rows = spectra_ref.shape[0]
    part = quarter_ref.shape[0]
    odd = place(held_ref)[3]
    start = pl.multiple_of(odd * (rows - part), 16)
    other = pl.multiple_of((1 - odd) * (rows - part), 16)
    rest = pltpu.make_async_copy(spectra_ref.at[pl.ds(other, part)], raw, sems.at[0])
    peptides = pltpu.make_async_copy(peptides_ref, held_ref, sems.at[1])
    rest.start()
    peptides.start()
    whole_ref[pl.ds(start, part), :] = quarter_ref[...]
    whole_ref[part : rows - part, :] = middle_ref[: rows - 2 * part, :]
    whole_ref[rows:, :] = middle_ref[rows - 2 * part :, :]
    rest.wait()
    process_into(raw, whole_ref.at[pl.ds(other, part)])
    peptides.wait()


def near_kernel(whole_ref, peptides_ref, best_ref):
    rows = best_ref.shape[1]
    bounds = read_note(whole_ref.at[rows:], rows)
    best_ref[...] = best_of(whole_ref[:rows, :], peptides_ref[...], bounds, place(peptides_ref)[0])


def last_kernel(
    direct_ref,
    relayed_ref,
    middle_ref,
    peptides_ref,
    own_ref,
    back_ref,
    out_ref,
    outer,
    far_best,
):
    part = direct_ref.shape[0]
    rows = own_ref.shape[1]
    far_best[...] = jnp.full(far_best.shape, LOWEST, jnp.float32)

    @pl.when(place(peptides_ref)[1])
    def _():
        odd = place(peptides_ref)[3]
        outer[pl.ds(pl.multiple_of(odd * part, 16), part), :] = direct_ref[...]
        outer[pl.ds(pl.multiple_of((1 - odd) * part, 16), part), :] = relayed_ref[...]
        count = rows - 2 * part
        bounds = read_note(middle_ref.at[count:], rows)
        first = place(peptides_ref)[0]
        inside = [bound[:, part : part + count] for bound in bounds]
        ends = [
            jnp.concatenate([bound[:, :part], bound[:, part + count :]], axis=1)
            for bound in bounds
        ]

        needed = meets(inside, peptides_ref)
        best = best_of(outer[...], peptides_ref[...], ends, first)
        far_best[:, :part] = best[:, :part]
        far_best[:, part + count :] = best[:, part:]

        @pl.when(needed)
        def _():
            far_best[:, part : part + count] = best_of(
                middle_ref[:count, :], peptides_ref[...], inside, first
            )

    near = jnp.maximum(own_ref[...], back_ref[...])
    half = (out_ref.shape[0] // 2, rows)
    lower = place(peptides_ref)[2]
    out_ref[: half[0]] = jnp.broadcast_to(jnp.where(lower, near, far_best[...]), half)
    out_ref[half[0] :] = jnp.broadcast_to(jnp.where(lower, far_best[...], near), half)


def in_hbm(array):
    return pltpu.with_memory_space_constraint(array, pltpu.HBM)


def call(kernel, out_shapes, in_specs, scratch, flops=1024):
    return pl.pallas_call(
        kernel,
        out_shape=[jax.ShapeDtypeStruct(shape, dtype) for shape, dtype in out_shapes],
        in_specs=in_specs,
        out_specs=[VMEM] * len(out_shapes),
        scratch_shapes=scratch,
        compiler_params=pltpu.CompilerParams(vmem_limit_bytes=20 * 2**20),
        cost_estimate=pl.CostEstimate(flops=flops, bytes_accessed=1024, transcendentals=0),
    )


def per_device(spectra, peptides, bounds):
    slabs, shards = lax.axis_size("mass"), lax.axis_size("pep")
    rows, bins = spectra.shape
    pep_rows = peptides.shape[0]
    part = rows // 4
    bf16, f32 = jnp.bfloat16, jnp.float32
    chip = [(i, i ^ 1) for i in range(slabs)]
    pairs = [(i, i + 1) for i in range(1, slabs - 1, 2)]
    across = pairs + [(high, low) for low, high in pairs]
    groups = [
        [i * shards + j for i in pair for j in range(shards)]
        for pair in pairs + [(0, slabs - 1)]
    ]
    relay = [
        (i * shards + j, i * shards + (j ^ beside(shards)[i % 2]))
        for i in range(1, slabs - 1)
        for j in range(shards)
    ]
    windows = bounds.T

    spectra, windows, peptides = in_hbm(spectra), in_hbm(windows), in_hbm(peptides)

    (quarter,) = call(
        quarter_kernel,
        [((part, bins), bf16)],
        [HBM],
        [pltpu.VMEM((part, bins), bf16), pltpu.SemaphoreType.DMA((2,))],
    )(spectra)
    direct = lax.ppermute(quarter, "mass", across)

    quarter, windows = lax.optimization_barrier((quarter, windows))
    (middle,) = call(
        middle_kernel,
        [((rows - 2 * part + NOTE, bins), bf16)],
        [HBM, HBM],
        [
            pltpu.VMEM((rows - 2 * part, bins), bf16),
            pltpu.VMEM(windows.shape, jnp.int32),
            pltpu.SemaphoreType.DMA((2,)),
        ],
    )(spectra, in_hbm(windows))
    far = lax.ppermute(middle, "mass", across)
    whole, held = call(
        whole_kernel,
        [((rows + NOTE, bins), bf16), (peptides.shape, bf16)],
        [HBM, HBM, VMEM, VMEM],
        [pltpu.VMEM((part, bins), bf16), pltpu.SemaphoreType.DMA((2,))],
    )(spectra, peptides, quarter, middle)

    score = [((1, rows), f32)], [VMEM, VMEM], []
    (own_best,) = call(near_kernel, *score, LONG)(whole, held)
    direct, whole = lax.optimization_barrier((direct, whole))
    near = lax.ppermute(whole, "mass", chip)
    relayed = lax.ppermute(direct, ("mass", "pep"), relay)
    near, own_best = lax.optimization_barrier((near, own_best))
    (near_best,) = call(near_kernel, *score)(near, held)
    back = lax.ppermute(near_best, "mass", chip)

    (bests,) = call(
        last_kernel,
        [((2 * shards, rows), f32)],
        [VMEM] * 6,
        [pltpu.VMEM((2 * part, bins), bf16), pltpu.VMEM((1, rows), f32)],
    )(direct, relayed, far, held, own_best, back)
    bests = lax.all_to_all(bests, ("mass", "pep"), 0, 0, axis_index_groups=groups)
    return jnp.max(bests, axis=0)


def solution(mesh):
    in_specs = (P("mass", None), P(("mass", "pep"), None), P("mass", None))
    out_specs = P("mass")
    return jax.shard_map(
        per_device, mesh=mesh, in_specs=in_specs, out_specs=out_specs, check_vma=False
    )
```

```python
import jax
import jax.numpy as jnp
from jax import lax
from jax.experimental import pallas as pl
from jax.experimental.pallas import tpu as pltpu
from jax.sharding import PartitionSpec as P

HALF_TAPS = 75
LOWEST = -1e30
ROW_BY_ROW = (((1,), (1,)), ((), ()))
VMEM = pl.BlockSpec(memory_space=pltpu.VMEM)
HBM = pl.BlockSpec(memory_space=pltpu.HBM)
BLOCK = 256
PAD = 128
NOTE = 8
LONG = 2**35
DIGITS = 3


def beside(shards):
    return 1, shards // 2


def place(peptides_ref):
    slabs, shards = lax.axis_size("mass"), lax.axis_size("pep")
    slab, shard = lax.axis_index("mass"), lax.axis_index("pep")
    inner = (slab > 0) & (slab < slabs - 1)
    lower = (slab == 0) | ((slab % 2 == 1) & inner)
    odd = (shard // beside(shards)[0] + shard // beside(shards)[1]) % 2
    return (slab * shards + shard) * peptides_ref.shape[0], inner, lower, odd


def process_into(rows_ref, out_ref):
    bins = rows_ref.shape[1]
    source = lax.broadcasted_iota(jnp.int32, (BLOCK + 2 * PAD, BLOCK), 0) - PAD
    target = lax.broadcasted_iota(jnp.int32, (BLOCK + 2 * PAD, BLOCK), 1)
    band = jnp.where(jnp.abs(source - target) <= HALF_TAPS, 1.0, 0.0).astype(jnp.bfloat16)
    for start in range(0, bins, BLOCK):
        low, high = max(start - PAD, 0), min(start + BLOCK + PAD, bins)
        skip = low - (start - PAD)
        window_sum = jnp.dot(
            rows_ref[:, low:high],
            band[skip : skip + high - low],
            preferred_element_type=jnp.float32,
        )
        values = rows_ref[:, start : start + BLOCK].astype(jnp.float32)
        out_ref[:, start : start + BLOCK] = (
            values - (window_sum - values) * (1.0 / (2.0 * HALF_TAPS))
        ).astype(jnp.bfloat16)


def best_of(processed, peptides, bounds, first):
    score = lax.dot_general(peptides, processed, ROW_BY_ROW, preferred_element_type=jnp.float32)
    index = lax.broadcasted_iota(jnp.int32, score.shape, 0)
    inside = (index >= bounds[0] - first) & (index <= bounds[1] - first)
    return jnp.max(jnp.where(inside, score, LOWEST), axis=0, keepdims=True)


def meets(bounds, peptides_ref):
    first = place(peptides_ref)[0]
    inside = (bounds[0] < first + peptides_ref.shape[0]) & (bounds[1] >= first)
    return jnp.max(inside.astype(jnp.int32)) > 0


def write_note(note_ref, bounds_ref):
    rows = bounds_ref.shape[1]
    row = lax.broadcasted_iota(jnp.int32, (NOTE, rows), 0)
    note = jnp.zeros((NOTE, rows), jnp.int32)
    for k in range(2):
        for d in range(DIGITS):
            digit = (bounds_ref[k : k + 1, :] >> (8 * d)) & 255
            note = jnp.where(row == k * DIGITS + d, digit, note)
    note_ref[...] = jnp.zeros(note_ref.shape, note_ref.dtype)
    note_ref[:, :rows] = note.astype(jnp.float32).astype(note_ref.dtype)


def read_note(note_ref, rows):
    note = note_ref[:, :rows].astype(jnp.float32).astype(jnp.int32)
    return [
        sum(note[k * DIGITS + d : k * DIGITS + d + 1, :] << (8 * d) for d in range(DIGITS))
        for k in range(2)
    ]


def quarter_kernel(spectra_ref, quarter_ref, raw, sems):
    part = quarter_ref.shape[0]
    start = place(spectra_ref)[3] * (spectra_ref.shape[0] - part)
    step = part // sems.shape[0]
    cuts = [(i * step, step) for i in range(sems.shape[0])]
    copies = [
        pltpu.make_async_copy(
            spectra_ref.at[pl.ds(pl.multiple_of(start + low, 16), size)],
            raw.at[low : low + size],
            sems.at[i],
        )
        for i, (low, size) in enumerate(cuts)
    ]
    for copy in copies:
        copy.start()
    for copy in copies:
        copy.wait()
    process_into(raw, quarter_ref)


def middle_kernel(spectra_ref, bounds_ref, middle_ref, raw, windows, sems):
    count = raw.shape[0]
    part = (spectra_ref.shape[0] - count) // 2
    rows = pltpu.make_async_copy(spectra_ref.at[part : part + count], raw, sems.at[0])
    bounds = pltpu.make_async_copy(bounds_ref, windows, sems.at[1])
    bounds.start()
    rows.start()
    bounds.wait()
    write_note(middle_ref.at[count:], windows)
    rows.wait()
    process_into(raw, middle_ref.at[:count])


def whole_kernel(
    spectra_ref, peptides_ref, quarter_ref, middle_ref, whole_ref, held_ref, raw, sems
):
    rows = spectra_ref.shape[0]
    part = quarter_ref.shape[0]
    odd = place(held_ref)[3]
    start = pl.multiple_of(odd * (rows - part), 16)
    other = pl.multiple_of((1 - odd) * (rows - part), 16)
    rest = pltpu.make_async_copy(spectra_ref.at[pl.ds(other, part)], raw, sems.at[0])
    peptides = pltpu.make_async_copy(peptides_ref, held_ref, sems.at[1])
    rest.start()
    peptides.start()
    whole_ref[pl.ds(start, part), :] = quarter_ref[...]
    whole_ref[part : rows - part, :] = middle_ref[: rows - 2 * part, :]
    whole_ref[rows:, :] = middle_ref[rows - 2 * part :, :]
    rest.wait()
    process_into(raw, whole_ref.at[pl.ds(other, part)])
    peptides.wait()


def near_kernel(whole_ref, peptides_ref, best_ref):
    rows = best_ref.shape[1]
    bounds = read_note(whole_ref.at[rows:], rows)
    best_ref[...] = best_of(whole_ref[:rows, :], peptides_ref[...], bounds, place(peptides_ref)[0])


def last_kernel(
    direct_ref,
    relayed_ref,
    middle_ref,
    peptides_ref,
    own_ref,
    back_ref,
    out_ref,
    outer,
    far_best,
):
    part = direct_ref.shape[0]
    rows = own_ref.shape[1]
    far_best[...] = jnp.full(far_best.shape, LOWEST, jnp.float32)

    @pl.when(place(peptides_ref)[1])
    def _():
        odd = place(peptides_ref)[3]
        outer[pl.ds(pl.multiple_of(odd * part, 16), part), :] = direct_ref[...]
        outer[pl.ds(pl.multiple_of((1 - odd) * part, 16), part), :] = relayed_ref[...]
        count = rows - 2 * part
        bounds = read_note(middle_ref.at[count:], rows)
        first = place(peptides_ref)[0]
        inside = [bound[:, part : part + count] for bound in bounds]
        ends = [
            jnp.concatenate([bound[:, :part], bound[:, part + count :]], axis=1)
            for bound in bounds
        ]

        needed = meets(inside, peptides_ref)
        best = best_of(outer[...], peptides_ref[...], ends, first)
        far_best[:, :part] = best[:, :part]
        far_best[:, part + count :] = best[:, part:]

        @pl.when(needed)
        def _():
            far_best[:, part : part + count] = best_of(
                middle_ref[:count, :], peptides_ref[...], inside, first
            )

    near = jnp.maximum(own_ref[...], back_ref[...])
    half = (out_ref.shape[0] // 2, rows)
    lower = place(peptides_ref)[2]
    out_ref[: half[0]] = jnp.broadcast_to(jnp.where(lower, near, far_best[...]), half)
    out_ref[half[0] :] = jnp.broadcast_to(jnp.where(lower, far_best[...], near), half)


def in_hbm(array):
    return pltpu.with_memory_space_constraint(array, pltpu.HBM)


def call(kernel, out_shapes, in_specs, scratch, flops=1024):
    return pl.pallas_call(
        kernel,
        out_shape=[jax.ShapeDtypeStruct(shape, dtype) for shape, dtype in out_shapes],
        in_specs=in_specs,
        out_specs=[VMEM] * len(out_shapes),
        scratch_shapes=scratch,
        compiler_params=pltpu.CompilerParams(vmem_limit_bytes=20 * 2**20),
        cost_estimate=pl.CostEstimate(flops=flops, bytes_accessed=1024, transcendentals=0),
    )


def per_device(spectra, peptides, bounds):
    slabs, shards = lax.axis_size("mass"), lax.axis_size("pep")
    rows, bins = spectra.shape
    pep_rows = peptides.shape[0]
    part = rows // 4
    bf16, f32 = jnp.bfloat16, jnp.float32
    chip = [(i, i ^ 1) for i in range(slabs)]
    pairs = [(i, i + 1) for i in range(1, slabs - 1, 2)]
    across = pairs + [(high, low) for low, high in pairs]
    groups = [
        [i * shards + j for i in pair for j in range(shards)]
        for pair in pairs + [(0, slabs - 1)]
    ]
    relay = [
        (i * shards + j, i * shards + (j ^ beside(shards)[i % 2]))
        for i in range(1, slabs - 1)
        for j in range(shards)
    ]
    windows = bounds.T

    spectra, windows, peptides = in_hbm(spectra), in_hbm(windows), in_hbm(peptides)

    (quarter,) = call(
        quarter_kernel,
        [((part, bins), bf16)],
        [HBM],
        [pltpu.VMEM((part, bins), bf16), pltpu.SemaphoreType.DMA((2,))],
    )(spectra)
    direct = lax.ppermute(quarter, "mass", across)

    quarter, windows = lax.optimization_barrier((quarter, windows))
    (middle,) = call(
        middle_kernel,
        [((rows - 2 * part + NOTE, bins), bf16)],
        [HBM, HBM],
        [
            pltpu.VMEM((rows - 2 * part, bins), bf16),
            pltpu.VMEM(windows.shape, jnp.int32),
            pltpu.SemaphoreType.DMA((2,)),
        ],
    )(spectra, in_hbm(windows))
    far = lax.ppermute(middle, "mass", across)
    whole, held = call(
        whole_kernel,
        [((rows + NOTE, bins), bf16), (peptides.shape, bf16)],
        [HBM, HBM, VMEM, VMEM],
        [pltpu.VMEM((part, bins), bf16), pltpu.SemaphoreType.DMA((2,))],
    )(spectra, peptides, quarter, middle)

    score = [((1, rows), f32)], [VMEM, VMEM], []
    (own_best,) = call(near_kernel, *score, LONG)(whole, held)
    near = lax.ppermute(whole, "mass", chip)
    relayed = lax.ppermute(direct, ("mass", "pep"), relay)
    near, own_best = lax.optimization_barrier((near, own_best))
    (near_best,) = call(near_kernel, *score)(near, held)
    back = lax.ppermute(near_best, "mass", chip)

    (bests,) = call(
        last_kernel,
        [((2 * shards, rows), f32)],
        [VMEM] * 6,
        [pltpu.VMEM((2 * part, bins), bf16), pltpu.VMEM((1, rows), f32)],
    )(direct, relayed, far, held, own_best, back)
    bests = lax.all_to_all(bests, ("mass", "pep"), 0, 0, axis_index_groups=groups)
    return jnp.max(bests, axis=0)


def solution(mesh):
    in_specs = (P("mass", None), P(("mass", "pep"), None), P("mass", None))
    out_specs = P("mass")
    return jax.shard_map(
        per_device, mesh=mesh, in_specs=in_specs, out_specs=out_specs, check_vma=False
    )
```

```python
import jax
import jax.numpy as jnp
from jax import lax
from jax.experimental import pallas as pl
from jax.experimental.pallas import tpu as pltpu
from jax.sharding import PartitionSpec as P

HALF_TAPS = 75
LOWEST = -1e30
ROW_BY_ROW = (((1,), (1,)), ((), ()))
VMEM = pl.BlockSpec(memory_space=pltpu.VMEM)
HBM = pl.BlockSpec(memory_space=pltpu.HBM)
BLOCK = 256
PAD = 128
NOTE = 8
LONG = 2**35
DIGITS = 3


def beside(shards):
    return 1, shards // 2


def place(peptides_ref):
    slabs, shards = lax.axis_size("mass"), lax.axis_size("pep")
    slab, shard = lax.axis_index("mass"), lax.axis_index("pep")
    inner = (slab > 0) & (slab < slabs - 1)
    lower = (slab == 0) | ((slab % 2 == 1) & inner)
    odd = (shard // beside(shards)[0] + shard // beside(shards)[1]) % 2
    return (slab * shards + shard) * peptides_ref.shape[0], inner, lower, odd


def process_into(rows_ref, out_ref):
    bins = rows_ref.shape[1]
    source = lax.broadcasted_iota(jnp.int32, (BLOCK + 2 * PAD, BLOCK), 0) - PAD
    target = lax.broadcasted_iota(jnp.int32, (BLOCK + 2 * PAD, BLOCK), 1)
    band = jnp.where(jnp.abs(source - target) <= HALF_TAPS, 1.0, 0.0).astype(jnp.bfloat16)
    for start in range(0, bins, BLOCK):
        low, high = max(start - PAD, 0), min(start + BLOCK + PAD, bins)
        skip = low - (start - PAD)
        window_sum = jnp.dot(
            rows_ref[:, low:high],
            band[skip : skip + high - low],
            preferred_element_type=jnp.float32,
        )
        values = rows_ref[:, start : start + BLOCK].astype(jnp.float32)
        out_ref[:, start : start + BLOCK] = (
            values - (window_sum - values) * (1.0 / (2.0 * HALF_TAPS))
        ).astype(jnp.bfloat16)


def best_of(processed, peptides, bounds, first):
    score = lax.dot_general(peptides, processed, ROW_BY_ROW, preferred_element_type=jnp.float32)
    index = lax.broadcasted_iota(jnp.int32, score.shape, 0)
    inside = (index >= bounds[0] - first) & (index <= bounds[1] - first)
    return jnp.max(jnp.where(inside, score, LOWEST), axis=0, keepdims=True)


def meets(bounds, peptides_ref):
    first = place(peptides_ref)[0]
    inside = (bounds[0] < first + peptides_ref.shape[0]) & (bounds[1] >= first)
    return jnp.max(inside.astype(jnp.int32)) > 0


def write_note(note_ref, bounds_ref):
    rows = bounds_ref.shape[1]
    row = lax.broadcasted_iota(jnp.int32, (NOTE, rows), 0)
    note = jnp.zeros((NOTE, rows), jnp.int32)
    for k in range(2):
        for d in range(DIGITS):
            digit = (bounds_ref[k : k + 1, :] >> (8 * d)) & 255
            note = jnp.where(row == k * DIGITS + d, digit, note)
    note_ref[...] = jnp.zeros(note_ref.shape, note_ref.dtype)
    note_ref[:, :rows] = note.astype(jnp.float32).astype(note_ref.dtype)


def read_note(note_ref, rows):
    note = note_ref[:, :rows].astype(jnp.float32).astype(jnp.int32)
    return [
        sum(note[k * DIGITS + d : k * DIGITS + d + 1, :] << (8 * d) for d in range(DIGITS))
        for k in range(2)
    ]


def quarter_kernel(spectra_ref, quarter_ref, sems):
    part = quarter_ref.shape[0]
    start = place(spectra_ref)[3] * (spectra_ref.shape[0] - part)
    step = part // sems.shape[0]
    cuts = [(i * step, step) for i in range(sems.shape[0])]
    copies = [
        pltpu.make_async_copy(
            spectra_ref.at[pl.ds(pl.multiple_of(start + low, 16), size)],
            quarter_ref.at[low : low + size],
            sems.at[i],
        )
        for i, (low, size) in enumerate(cuts)
    ]
    for copy in copies:
        copy.start()
    for copy in copies:
        copy.wait()


def process_kernel(rows_ref, processed_ref):
    process_into(rows_ref, processed_ref)


def middle_kernel(spectra_ref, bounds_ref, middle_ref, raw, windows, sems):
    count = raw.shape[0]
    part = (spectra_ref.shape[0] - count) // 2
    rows = pltpu.make_async_copy(spectra_ref.at[part : part + count], raw, sems.at[0])
    bounds = pltpu.make_async_copy(bounds_ref, windows, sems.at[1])
    bounds.start()
    rows.start()
    bounds.wait()
    write_note(middle_ref.at[count:], windows)
    rows.wait()
    process_into(raw, middle_ref.at[:count])


def whole_kernel(
    spectra_ref, peptides_ref, quarter_ref, middle_ref, whole_ref, held_ref, raw, sems
):
    rows = spectra_ref.shape[0]
    part = quarter_ref.shape[0]
    odd = place(held_ref)[3]
    start = pl.multiple_of(odd * (rows - part), 16)
    other = pl.multiple_of((1 - odd) * (rows - part), 16)
    rest = pltpu.make_async_copy(spectra_ref.at[pl.ds(other, part)], raw, sems.at[0])
    peptides = pltpu.make_async_copy(peptides_ref, held_ref, sems.at[1])
    rest.start()
    peptides.start()
    process_into(quarter_ref, whole_ref.at[pl.ds(start, part)])
    whole_ref[part : rows - part, :] = middle_ref[: rows - 2 * part, :]
    whole_ref[rows:, :] = middle_ref[rows - 2 * part :, :]
    rest.wait()
    process_into(raw, whole_ref.at[pl.ds(other, part)])
    peptides.wait()


def near_kernel(whole_ref, peptides_ref, best_ref):
    rows = best_ref.shape[1]
    bounds = read_note(whole_ref.at[rows:], rows)
    best_ref[...] = best_of(whole_ref[:rows, :], peptides_ref[...], bounds, place(peptides_ref)[0])


def last_kernel(
    direct_ref,
    relayed_ref,
    middle_ref,
    peptides_ref,
    own_ref,
    back_ref,
    out_ref,
    outer,
    far_best,
):
    part = direct_ref.shape[0]
    rows = own_ref.shape[1]
    far_best[...] = jnp.full(far_best.shape, LOWEST, jnp.float32)

    @pl.when(place(peptides_ref)[1])
    def _():
        odd = place(peptides_ref)[3]
        outer[pl.ds(pl.multiple_of(odd * part, 16), part), :] = direct_ref[...]
        outer[pl.ds(pl.multiple_of((1 - odd) * part, 16), part), :] = relayed_ref[...]
        count = rows - 2 * part
        bounds = read_note(middle_ref.at[count:], rows)
        first = place(peptides_ref)[0]
        inside = [bound[:, part : part + count] for bound in bounds]
        ends = [
            jnp.concatenate([bound[:, :part], bound[:, part + count :]], axis=1)
            for bound in bounds
        ]

        needed = meets(inside, peptides_ref)
        best = best_of(outer[...], peptides_ref[...], ends, first)
        far_best[:, :part] = best[:, :part]
        far_best[:, part + count :] = best[:, part:]

        @pl.when(needed)
        def _():
            far_best[:, part : part + count] = best_of(
                middle_ref[:count, :], peptides_ref[...], inside, first
            )

    near = jnp.maximum(own_ref[...], back_ref[...])
    half = (out_ref.shape[0] // 2, rows)
    lower = place(peptides_ref)[2]
    out_ref[: half[0]] = jnp.broadcast_to(jnp.where(lower, near, far_best[...]), half)
    out_ref[half[0] :] = jnp.broadcast_to(jnp.where(lower, far_best[...], near), half)


def in_hbm(array):
    return pltpu.with_memory_space_constraint(array, pltpu.HBM)


def call(kernel, out_shapes, in_specs, scratch, flops=1024):
    return pl.pallas_call(
        kernel,
        out_shape=[jax.ShapeDtypeStruct(shape, dtype) for shape, dtype in out_shapes],
        in_specs=in_specs,
        out_specs=[VMEM] * len(out_shapes),
        scratch_shapes=scratch,
        compiler_params=pltpu.CompilerParams(vmem_limit_bytes=20 * 2**20),
        cost_estimate=pl.CostEstimate(flops=flops, bytes_accessed=1024, transcendentals=0),
    )


def per_device(spectra, peptides, bounds):
    slabs, shards = lax.axis_size("mass"), lax.axis_size("pep")
    rows, bins = spectra.shape
    pep_rows = peptides.shape[0]
    part = rows // 4
    bf16, f32 = jnp.bfloat16, jnp.float32
    chip = [(i, i ^ 1) for i in range(slabs)]
    pairs = [(i, i + 1) for i in range(1, slabs - 1, 2)]
    across = pairs + [(high, low) for low, high in pairs]
    groups = [
        [i * shards + j for i in pair for j in range(shards)]
        for pair in pairs + [(0, slabs - 1)]
    ]
    relay = [
        (i * shards + j, i * shards + (j ^ beside(shards)[i % 2]))
        for i in range(1, slabs - 1)
        for j in range(shards)
    ]
    windows = bounds.T

    spectra, windows, peptides = in_hbm(spectra), in_hbm(windows), in_hbm(peptides)

    (quarter,) = call(
        quarter_kernel,
        [((part, bins), bf16)],
        [HBM],
        [pltpu.SemaphoreType.DMA((2,))],
    )(spectra)
    direct = lax.ppermute(quarter, "mass", across)

    quarter, windows = lax.optimization_barrier((quarter, windows))
    (middle,) = call(
        middle_kernel,
        [((rows - 2 * part + NOTE, bins), bf16)],
        [HBM, HBM],
        [
            pltpu.VMEM((rows - 2 * part, bins), bf16),
            pltpu.VMEM(windows.shape, jnp.int32),
            pltpu.SemaphoreType.DMA((2,)),
        ],
    )(spectra, in_hbm(windows))
    far = lax.ppermute(middle, "mass", across)
    whole, held = call(
        whole_kernel,
        [((rows + NOTE, bins), bf16), (peptides.shape, bf16)],
        [HBM, HBM, VMEM, VMEM],
        [pltpu.VMEM((part, bins), bf16), pltpu.SemaphoreType.DMA((2,))],
    )(spectra, peptides, quarter, middle)

    score = [((1, rows), f32)], [VMEM, VMEM], []
    (own_best,) = call(near_kernel, *score, LONG)(whole, held)
    near = lax.ppermute(whole, "mass", chip)
    relayed = lax.ppermute(direct, ("mass", "pep"), relay)
    (direct,) = call(process_kernel, [((part, bins), bf16)], [VMEM], [])(direct)
    near, own_best, direct = lax.optimization_barrier((near, own_best, direct))
    (near_best,) = call(near_kernel, *score)(near, held)
    back = lax.ppermute(near_best, "mass", chip)
    relayed, near_best = lax.optimization_barrier((relayed, near_best))
    (relayed,) = call(process_kernel, [((part, bins), bf16)], [VMEM], [])(relayed)
    far, relayed = lax.optimization_barrier((far, relayed))

    (bests,) = call(
        last_kernel,
        [((2 * shards, rows), f32)],
        [VMEM] * 6,
        [pltpu.VMEM((2 * part, bins), bf16), pltpu.VMEM((1, rows), f32)],
    )(direct, relayed, far, held, own_best, back)
    bests = lax.all_to_all(bests, ("mass", "pep"), 0, 0, axis_index_groups=groups)
    return jnp.max(bests, axis=0)


def solution(mesh):
    in_specs = (P("mass", None), P(("mass", "pep"), None), P("mass", None))
    out_specs = P("mass")
    return jax.shard_map(
        per_device, mesh=mesh, in_specs=in_specs, out_specs=out_specs, check_vma=False
    )
```

```python
import jax
import jax.numpy as jnp
from jax import lax
from jax.experimental import pallas as pl
from jax.experimental.pallas import tpu as pltpu
from jax.sharding import PartitionSpec as P

HALF_TAPS = 75
LOWEST = -1e30
ROW_BY_ROW = (((1,), (1,)), ((), ()))
VMEM = pl.BlockSpec(memory_space=pltpu.VMEM)
HBM = pl.BlockSpec(memory_space=pltpu.HBM)
BLOCK = 256
PAD = 128
NOTE = 16
LONG = 2**35
DIGITS = 3


def beside(shards):
    return 1, shards // 2


def place(peptides_ref):
    slabs, shards = lax.axis_size("mass"), lax.axis_size("pep")
    slab, shard = lax.axis_index("mass"), lax.axis_index("pep")
    inner = (slab > 0) & (slab < slabs - 1)
    lower = (slab == 0) | ((slab % 2 == 1) & inner)
    odd = (shard // beside(shards)[0] + shard // beside(shards)[1]) % 2
    return (slab * shards + shard) * peptides_ref.shape[0], inner, lower, odd


def process_into(rows_ref, out_ref):
    bins = rows_ref.shape[1]
    source = lax.broadcasted_iota(jnp.int32, (BLOCK + 2 * PAD, BLOCK), 0) - PAD
    target = lax.broadcasted_iota(jnp.int32, (BLOCK + 2 * PAD, BLOCK), 1)
    band = jnp.where(jnp.abs(source - target) <= HALF_TAPS, 1.0, 0.0).astype(jnp.bfloat16)
    for start in range(0, bins, BLOCK):
        low, high = max(start - PAD, 0), min(start + BLOCK + PAD, bins)
        skip = low - (start - PAD)
        window_sum = jnp.dot(
            rows_ref[:, low:high],
            band[skip : skip + high - low],
            preferred_element_type=jnp.float32,
        )
        values = rows_ref[:, start : start + BLOCK].astype(jnp.float32)
        out_ref[:, start : start + BLOCK] = (
            values - (window_sum - values) * (1.0 / (2.0 * HALF_TAPS))
        ).astype(jnp.bfloat16)


def best_of(processed, peptides, bounds, first):
    score = lax.dot_general(peptides, processed, ROW_BY_ROW, preferred_element_type=jnp.float32)
    index = lax.broadcasted_iota(jnp.int32, score.shape, 0)
    inside = (index >= bounds[0] - first) & (index <= bounds[1] - first)
    return jnp.max(jnp.where(inside, score, LOWEST), axis=0, keepdims=True)


def meets(bounds, peptides_ref):
    first = place(peptides_ref)[0]
    inside = (bounds[0] < first + peptides_ref.shape[0]) & (bounds[1] >= first)
    return jnp.max(inside.astype(jnp.int32)) > 0


def write_note(note_ref, bounds_ref):
    rows = bounds_ref.shape[1]
    row = lax.broadcasted_iota(jnp.int32, (NOTE, rows), 0)
    note = jnp.zeros((NOTE, rows), jnp.int32)
    for k in range(2):
        for d in range(DIGITS):
            digit = (bounds_ref[k : k + 1, :] >> (8 * d)) & 255
            note = jnp.where(row == k * DIGITS + d, digit, note)
    note_ref[...] = jnp.zeros(note_ref.shape, note_ref.dtype)
    note_ref[:, :rows] = note.astype(jnp.float32).astype(note_ref.dtype)


def read_note(note_ref, rows):
    note = note_ref[:, :rows].astype(jnp.float32).astype(jnp.int32)
    return [
        sum(note[k * DIGITS + d : k * DIGITS + d + 1, :] << (8 * d) for d in range(DIGITS))
        for k in range(2)
    ]


def quarter_kernel(spectra_ref, quarter_ref, sems):
    part = quarter_ref.shape[0]
    start = place(spectra_ref)[3] * (spectra_ref.shape[0] - part)
    step = part // sems.shape[0]
    cuts = [(i * step, step) for i in range(sems.shape[0])]
    copies = [
        pltpu.make_async_copy(
            spectra_ref.at[pl.ds(pl.multiple_of(start + low, 16), size)],
            quarter_ref.at[low : low + size],
            sems.at[i],
        )
        for i, (low, size) in enumerate(cuts)
    ]
    for copy in copies:
        copy.start()
    for copy in copies:
        copy.wait()


def process_kernel(rows_ref, processed_ref):
    process_into(rows_ref, processed_ref)


def middle_kernel(spectra_ref, bounds_ref, middle_ref, raw, windows, sems):
    count = raw.shape[0]
    part = (spectra_ref.shape[0] - count) // 2
    rows = pltpu.make_async_copy(spectra_ref.at[part : part + count], raw, sems.at[0])
    bounds = pltpu.make_async_copy(bounds_ref, windows, sems.at[1])
    bounds.start()
    rows.start()
    bounds.wait()
    write_note(middle_ref.at[count:], windows)
    rows.wait()
    process_into(raw, middle_ref.at[:count])


def whole_kernel(
    spectra_ref, peptides_ref, quarter_ref, middle_ref, whole_ref, held_ref, raw, sems
):
    rows = spectra_ref.shape[0]
    part = quarter_ref.shape[0]
    odd = place(held_ref)[3]
    start = pl.multiple_of(odd * (rows - part), 16)
    other = pl.multiple_of((1 - odd) * (rows - part), 16)
    rest = pltpu.make_async_copy(spectra_ref.at[pl.ds(other, part)], raw, sems.at[0])
    peptides = pltpu.make_async_copy(peptides_ref, held_ref, sems.at[1])
    rest.start()
    peptides.start()
    process_into(quarter_ref, whole_ref.at[pl.ds(start, part)])
    whole_ref[part : rows - part, :] = middle_ref[: rows - 2 * part, :]
    whole_ref[rows:, :] = middle_ref[rows - 2 * part :, :]
    rest.wait()
    process_into(raw, whole_ref.at[pl.ds(other, part)])
    peptides.wait()


def near_kernel(whole_ref, peptides_ref, best_ref):
    rows = best_ref.shape[1]
    bounds = read_note(whole_ref.at[rows:], rows)
    best_ref[...] = best_of(whole_ref[:rows, :], peptides_ref[...], bounds, place(peptides_ref)[0])


def last_kernel(
    direct_ref,
    relayed_ref,
    middle_ref,
    peptides_ref,
    own_ref,
    back_ref,
    out_ref,
    outer,
    far_best,
):
    part = direct_ref.shape[0]
    rows = own_ref.shape[1]
    far_best[...] = jnp.full(far_best.shape, LOWEST, jnp.float32)

    @pl.when(place(peptides_ref)[1])
    def _():
        odd = place(peptides_ref)[3]
        outer[pl.ds(pl.multiple_of(odd * part, 16), part), :] = direct_ref[...]
        outer[pl.ds(pl.multiple_of((1 - odd) * part, 16), part), :] = relayed_ref[...]
        count = rows - 2 * part
        bounds = read_note(middle_ref.at[count:], rows)
        first = place(peptides_ref)[0]
        inside = [bound[:, part : part + count] for bound in bounds]
        ends = [
            jnp.concatenate([bound[:, :part], bound[:, part + count :]], axis=1)
            for bound in bounds
        ]

        needed = meets(inside, peptides_ref)
        best = best_of(outer[...], peptides_ref[...], ends, first)
        far_best[:, :part] = best[:, :part]
        far_best[:, part + count :] = best[:, part:]

        @pl.when(needed)
        def _():
            far_best[:, part : part + count] = best_of(
                middle_ref[:count, :], peptides_ref[...], inside, first
            )

    near = jnp.maximum(own_ref[...], back_ref[...])
    half = (out_ref.shape[0] // 2, rows)
    lower = place(peptides_ref)[2]
    out_ref[: half[0]] = jnp.broadcast_to(jnp.where(lower, near, far_best[...]), half)
    out_ref[half[0] :] = jnp.broadcast_to(jnp.where(lower, far_best[...], near), half)


def in_hbm(array):
    return pltpu.with_memory_space_constraint(array, pltpu.HBM)


def call(kernel, out_shapes, in_specs, scratch, flops=1024):
    return pl.pallas_call(
        kernel,
        out_shape=[jax.ShapeDtypeStruct(shape, dtype) for shape, dtype in out_shapes],
        in_specs=in_specs,
        out_specs=[VMEM] * len(out_shapes),
        scratch_shapes=scratch,
        compiler_params=pltpu.CompilerParams(vmem_limit_bytes=20 * 2**20),
        cost_estimate=pl.CostEstimate(flops=flops, bytes_accessed=1024, transcendentals=0),
    )


def per_device(spectra, peptides, bounds):
    slabs, shards = lax.axis_size("mass"), lax.axis_size("pep")
    rows, bins = spectra.shape
    pep_rows = peptides.shape[0]
    part = rows // 4
    bf16, f32 = jnp.bfloat16, jnp.float32
    chip = [(i, i ^ 1) for i in range(slabs)]
    pairs = [(i, i + 1) for i in range(1, slabs - 1, 2)]
    across = pairs + [(high, low) for low, high in pairs]
    groups = [
        [i * shards + j for i in pair for j in range(shards)]
        for pair in pairs + [(0, slabs - 1)]
    ]
    relay = [
        (i * shards + j, i * shards + (j ^ beside(shards)[i % 2]))
        for i in range(1, slabs - 1)
        for j in range(shards)
    ]
    windows = bounds.T

    spectra, windows, peptides = in_hbm(spectra), in_hbm(windows), in_hbm(peptides)

    (quarter,) = call(
        quarter_kernel,
        [((part, bins), bf16)],
        [HBM],
        [pltpu.SemaphoreType.DMA((2,))],
    )(spectra)
    direct = lax.ppermute(quarter, "mass", across)

    quarter, windows = lax.optimization_barrier((quarter, windows))
    (middle,) = call(
        middle_kernel,
        [((rows - 2 * part + NOTE, bins), bf16)],
        [HBM, HBM],
        [
            pltpu.VMEM((rows - 2 * part, bins), bf16),
            pltpu.VMEM(windows.shape, jnp.int32),
            pltpu.SemaphoreType.DMA((2,)),
        ],
    )(spectra, in_hbm(windows))
    far = lax.ppermute(middle, "mass", across)
    whole, held = call(
        whole_kernel,
        [((rows + NOTE, bins), bf16), (peptides.shape, bf16)],
        [HBM, HBM, VMEM, VMEM],
        [pltpu.VMEM((part, bins), bf16), pltpu.SemaphoreType.DMA((2,))],
    )(spectra, peptides, quarter, middle)

    score = [((1, rows), f32)], [VMEM, VMEM], []
    (own_best,) = call(near_kernel, *score, LONG)(whole, held)
    near = lax.ppermute(whole, "mass", chip)
    relayed = lax.ppermute(direct, ("mass", "pep"), relay)
    (direct,) = call(process_kernel, [((part, bins), bf16)], [VMEM], [])(direct)
    near, own_best, direct = lax.optimization_barrier((near, own_best, direct))
    (near_best,) = call(near_kernel, *score)(near, held)
    back = lax.ppermute(near_best, "mass", chip)
    relayed, near_best = lax.optimization_barrier((relayed, near_best))
    (relayed,) = call(process_kernel, [((part, bins), bf16)], [VMEM], [])(relayed)
    far, relayed = lax.optimization_barrier((far, relayed))

    (bests,) = call(
        last_kernel,
        [((2 * shards, rows), f32)],
        [VMEM] * 6,
        [pltpu.VMEM((2 * part, bins), bf16), pltpu.VMEM((1, rows), f32)],
    )(direct, relayed, far, held, own_best, back)
    bests = lax.all_to_all(bests, ("mass", "pep"), 0, 0, axis_index_groups=groups)
    return jnp.max(bests, axis=0)


def solution(mesh):
    in_specs = (P("mass", None), P(("mass", "pep"), None), P("mass", None))
    out_specs = P("mass")
    return jax.shard_map(
        per_device, mesh=mesh, in_specs=in_specs, out_specs=out_specs, check_vma=False
    )
```
